256 devices in a mesh: site: 32 (over z, y_hi, core), dp: 8 (over x, y_lo).
Axes of the slice: x: 4, y: 4 (y_hi: 2, y_lo: 2; y = y_hi * 2 + y_lo), z: 8, core: 2. Of those that a mesh axis runs over, the one named last changes fastest.
Arguments:
- image_embed: bfloat16 [32768, 1152], P(('site', 'dp')), may hold values from -0.3 to 0.3
- text_embed: bfloat16 [32768, 1152], P(('site', 'dp')), may hold values from -0.3 to 0.3
- log_sharpness_factor: float32 [], replicated, may hold values from 1.5 to 3
- couple_score_shift: float32 [], replicated, may hold values from -4 to 0
Outputs:
- pair_loss: float32 [], replicated
- grad_image: float32 [32768, 1152], P(('site', 'dp'))
- grad_text: float32 [32768, 1152], P(('site', 'dp'))
The draws below stay inside these ranges and needn't reach their ends.
All inputs are finite; a program needn't handle non-finite values.
Results may differ from the reference program's by a relative error of at most 0.00077.
Values may be sent and summed in bfloat16 or wider, within the bound.
No kernel may reach another device: no remote copies, remote signals or barrier semaphores. Data moves between devices by JAX's collectives and lax.ppermute only.
A program may use at most 128 MiB of HBM per device.

```python
import jax
import jax.numpy as jnp
from jax import lax

D = 1152
ROWS = 128
BAND = 4
PAIRS = 32768
N_SITE = 32
N_DP = 8


def shared_direction(key):
    return jax.random.normal(jax.random.fold_in(key, 101), (1, D), jnp.float32)


def mixed_rows(key, direction, power):
    position = jnp.arange(PAIRS, dtype=jnp.float32)[:, None] / jnp.float32(PAIRS)
    weight = 0.05 + 0.6 * position ** power
    noise = jnp.clip(jax.random.normal(key, (PAIRS, D), jnp.float32), -6.0, 6.0)
    values = 0.03 * (jnp.sqrt(1.0 - weight * weight) * noise + weight * direction)
    return jnp.clip(values, -0.3, 0.3)


def draw_image_embed(key, part):
    direction = shared_direction(key)
    key = jax.random.fold_in(key, 7)
    return mixed_rows(key, direction, 1.0).astype(jnp.bfloat16)


def draw_text_embed(key, part):
    direction = shared_direction(key)
    key = jax.random.fold_in(key, 13)
    return mixed_rows(key, direction, 1.0).astype(jnp.bfloat16)


def setup_inputs(seed: int = 0) -> dict:
    keys = jax.random.split(jax.random.key(seed), 5)
    return {
        "image_embed": draw_image_embed(jax.random.fold_in(keys[4], 71), 0),
        "text_embed": draw_text_embed(jax.random.fold_in(keys[4], 71), 0),
        "log_sharpness_factor": jnp.clip(jax.random.uniform(keys[2], (), jnp.float32, 1.5, 3.0), 1.5, 3.0),
        "couple_score_shift": jnp.clip(jax.random.uniform(keys[3], (), jnp.float32, -4.0, 0.0), -4.0, 0.0),
    }


EPS = 1e-06

def normalize(embed):
    values = embed.astype(jnp.float32)
    inverse = lax.rsqrt(lax.optimization_barrier(jnp.sum(values * values, axis=-1, keepdims=True)) + EPS)
    return (values, inverse)

def back_norm(values, inverse, upstream):
    inner = lax.optimization_barrier(jnp.sum(values * upstream, axis=-1, keepdims=True))
    return inverse * upstream - inverse * inverse * inverse * values * inner

def reference(image_embed, text_embed, log_sharpness_factor, couple_score_shift):
    group_rows = N_DP * ROWS
    img_values, img_inverse = normalize(image_embed)
    txt_values, txt_inverse = normalize(text_embed)
    img_unit = (img_values * img_inverse).astype(jnp.bfloat16)
    txt_unit = (txt_values * txt_inverse).astype(jnp.bfloat16)
    sharpness_factor = jnp.exp(log_sharpness_factor)
    img_groups = img_unit.reshape(N_SITE, group_rows, D)
    txt_groups = txt_unit.reshape(N_SITE, group_rows, D)
    band_text = jnp.stack([jnp.roll(txt_groups, -segment_shift_amount, axis=0) for segment_shift_amount in range(BAND)], 1)
    positive = (jnp.arange(group_rows)[:, None] == jnp.arange(group_rows)[None, :]).astype(jnp.float32)

    def per_group(inputs):
        picture_sample_count, caption_sample_count = inputs
        loss_sum = jnp.zeros((), jnp.float32)
        img_grad = jnp.zeros((group_rows, D), jnp.float32)
        txt_terms = []
        for segment_shift_amount in range(BAND):
            couple_score_matrix = sharpness_factor * jnp.dot(picture_sample_count, caption_sample_count[segment_shift_amount].T, preferred_element_type=jnp.float32) + couple_score_shift
            couple_match_sign = positive if segment_shift_amount == 0 else jnp.zeros_like(positive)
            label = 2.0 * couple_match_sign - 1.0
            loss_sum = loss_sum + jnp.sum(jax.nn.softplus(-label * couple_score_matrix))
            couple_weight_entry = (sharpness_factor * (jax.nn.sigmoid(couple_score_matrix) - couple_match_sign)).astype(jnp.bfloat16)
            img_grad = img_grad + jnp.dot(couple_weight_entry, caption_sample_count[segment_shift_amount], preferred_element_type=jnp.float32)
            txt_terms.append(jnp.dot(couple_weight_entry.T, picture_sample_count, preferred_element_type=jnp.float32))
        return (loss_sum, img_grad, jnp.stack(txt_terms, 0))
    loss_sums, img_grads, txt_terms = lax.map(per_group, (img_groups, band_text))
    txt_grad = txt_terms[:, 0]
    for segment_shift_amount in range(1, BAND):
        txt_grad = txt_grad + jnp.roll(txt_terms[:, segment_shift_amount], segment_shift_amount, axis=0)
    pair_loss = jnp.sum(loss_sums) / jnp.float32(PAIRS * BAND * group_rows)
    grad_image = back_norm(img_values, img_inverse, img_grads.reshape(PAIRS, D))
    grad_text = back_norm(txt_values, txt_inverse, txt_grad.reshape(PAIRS, D))
    return (pair_loss, grad_image, grad_text)
```

```python
import functools

import jax
import jax.numpy as jnp
from jax import lax
from jax.experimental import pallas as pl
from jax.experimental.pallas import tpu as pltpu
from jax.sharding import PartitionSpec as P

BAND = 4
EPS = 1e-06
AXES = ("site", "dp")
Z, YH, CORE, X, YL = 8, 2, 2, 4, 2


def route(move):
    pairs = []
    for source in range(Z * YH * CORE * X * YL):
        rest, yl = divmod(source, YL)
        rest, x = divmod(rest, X)
        rest, core = divmod(rest, CORE)
        z, yh = divmod(rest, YH)
        z, yh, core, x, yl = move(z, yh, core, x, yl)
        target = ((((z % Z) * YH + yh) * CORE + core) * X + x % X) * YL + yl
        pairs.append((source, target))
    return pairs


UP_X = route(lambda z, yh, c, x, yl: (z, yh, c, x + 1, yl))
DOWN_X = route(lambda z, yh, c, x, yl: (z, yh, c, x - 1, yl))
MATE_Y = route(lambda z, yh, c, x, yl: (z, yh, c, x, 1 - yl))
FLIP_Y = route(lambda z, yh, c, x, yl: (z, 1 - yh, c, x, 1 - yl))
DOWN_Z = route(lambda z, yh, c, x, yl: (z - 1, yh, c, x, yl))
UP_Z = route(lambda z, yh, c, x, yl: (z + 1, yh, c, x, yl))
OTHER_CORE = route(lambda z, yh, c, x, yl: (z, yh, 1 - c, x, yl))
LOSS_ROUTES = (
    OTHER_CORE,
    route(lambda z, yh, c, x, yl: (z, yh, c, x ^ 1, yl)),
    route(lambda z, yh, c, x, yl: (z, yh, c, 3 - x, yl)),
    MATE_Y,
    FLIP_Y,
    route(lambda z, yh, c, x, yl: (z ^ 1, yh, c, x, yl)),
    route(lambda z, yh, c, x, yl: (z ^ 2, yh, c, x, yl)),
    route(lambda z, yh, c, x, yl: (z ^ 4, yh, c, x, yl)),
)


def move(block, pairs):
    return lax.ppermute(block, AXES, pairs)


def unit_kernel(image_ref, text_ref, img_unit_ref, txt_unit_ref):
    for source, unit in ((image_ref, img_unit_ref), (text_ref, txt_unit_ref)):
        values = source[...].astype(jnp.float32)
        inverse = lax.rsqrt(jnp.sum(values * values, axis=-1, keepdims=True) + EPS)
        unit[...] = (values * inverse).astype(jnp.bfloat16)


def units(image_embed, text_embed):
    out = jax.ShapeDtypeStruct(image_embed.shape, jnp.bfloat16)
    return pl.pallas_call(unit_kernel, out_shape=(out, out))(image_embed, text_embed)


def pair_kernel(rows, img_sizes, *refs):
    scalars_ref, refs = refs[0], refs[1:]
    img_refs, refs = refs[: len(img_sizes)], refs[len(img_sizes) :]
    txt_refs, refs = refs[:BAND], refs[BAND:]
    img_grad_ref, txt_grad_ref, loss_ref, img, txt = refs
    start = 0
    for ref, size in zip(img_refs, img_sizes):
        img[start : start + size, :] = ref[...]
        start += size
    for k, ref in enumerate(txt_refs):
        txt[k * rows : (k + 1) * rows, :] = ref[...]
    sharpness = scalars_ref[0]
    shift = scalars_ref[1]
    chunk = 2 * rows
    txt_grad_ref[...] = jnp.zeros_like(txt_grad_ref)
    loss_ref[...] = jnp.zeros_like(loss_ref)

    def step(i, carry):
        block = pl.ds(pl.multiple_of(i * chunk, chunk), chunk)
        images = img[block, :]
        score = sharpness * lax.dot_general(
            images, txt[...], (((1,), (1,)), ((), ())), preferred_element_type=jnp.float32
        ) + shift
        row = lax.broadcasted_iota(jnp.int32, score.shape, 0) + i * chunk
        column = lax.broadcasted_iota(jnp.int32, score.shape, 1)
        positive = jnp.logical_and(row == column, row < rows)
        decay = jnp.exp(-jnp.abs(score))
        softplus = jnp.maximum(jnp.where(positive, -score, score), 0.0) + jnp.log1p(decay)
        weight = jnp.where(score >= 0, 1.0, decay) / (1.0 + decay)
        weight = sharpness * (weight - jnp.where(positive, 1.0, 0.0))
        weight = weight.astype(jnp.bfloat16)
        loss_ref[...] += jnp.sum(softplus.reshape(-1, 8, softplus.shape[1]), axis=0)
        img_grad_ref[block, :] = jnp.dot(weight, txt[...], preferred_element_type=jnp.float32)
        txt_grad_ref[...] += lax.dot_general(
            weight, images, (((0,), (0,)), ((), ())), preferred_element_type=jnp.float32
        )
        return carry

    lax.fori_loop(0, img.shape[0] // chunk, step, 0)


def pair_terms(scalars, images, texts):
    rows, width = texts[0].shape
    sizes = tuple(block.shape[0] for block in images)
    total = sum(sizes)
    vmem = pl.BlockSpec(memory_space=pltpu.VMEM)
    return pl.pallas_call(
        functools.partial(pair_kernel, rows, sizes),
        out_shape=(
            jax.ShapeDtypeStruct((total, width), jnp.float32),
            jax.ShapeDtypeStruct((BAND * rows, width), jnp.float32),
            jax.ShapeDtypeStruct((8, BAND * rows), jnp.float32),
        ),
        in_specs=[pl.BlockSpec(memory_space=pltpu.SMEM)] + [vmem] * (len(images) + len(texts)),
        out_specs=(vmem, vmem, vmem),
        scratch_shapes=[
            pltpu.VMEM((total, width), jnp.bfloat16),
            pltpu.VMEM((BAND * rows, width), jnp.bfloat16),
        ],
        compiler_params=pltpu.CompilerParams(vmem_limit_bytes=56 * 1024 * 1024),
    )(scalars, *images, *texts)


def back_norm(embed, upstream):
    values = embed.astype(jnp.float32)
    inverse = lax.rsqrt(jnp.sum(values * values, axis=-1, keepdims=True) + EPS)
    inner = jnp.sum(values * upstream, axis=-1, keepdims=True)
    return inverse * upstream - inverse * inverse * inverse * values * inner


def narrow(block):
    return block.astype(jnp.float16)


def wide(block):
    return block.astype(jnp.float32)


def shards(image_embed, text_embed, log_sharpness_factor, couple_score_shift):
    rows = image_embed.shape[0]
    half = rows // 2
    site = lax.axis_index("site")
    second = (site % CORE) == 1
    upper = (site // CORE) % YH == 1
    scalars = jnp.stack([jnp.exp(log_sharpness_factor), couple_score_shift])
    own_img, own_txt = units(image_embed, text_embed)

    z_txt = move(own_txt, DOWN_Z)
    img_a = move(own_img, UP_X)
    img_b = move(own_img, DOWN_X)
    img_m = move(own_img, MATE_Y)
    y_txt = move(jnp.where(upper, own_txt, z_txt), FLIP_Y)
    img_2a = move(img_b[:half], DOWN_X)
    img_2b = move(img_a[half:], UP_X)
    img_ma = move(img_m, UP_X)
    img_mb = move(img_m, DOWN_X)
    img_m2a = move(img_2a, MATE_Y)
    img_m2b = move(img_2b, MATE_Y)
    c_txt = move(jnp.where(second, own_txt, z_txt), OTHER_CORE)
    d_txt = move(y_txt, OTHER_CORE)

    images = (own_img, img_a, img_b, img_m, img_2a, img_2b, img_ma, img_mb, img_m2a, img_m2b)
    texts = (own_txt, c_txt, y_txt, d_txt)
    img_terms, txt_terms, loss_part = pair_terms(scalars, images, texts)
    of_own, of_a, of_b, of_m, of_2, of_ma, of_mb, of_m2 = (
        img_terms[i * rows : (i + 1) * rows] for i in range(8)
    )
    of_txt, of_c, of_y, of_d = (txt_terms[i * rows : (i + 1) * rows] for i in range(4))

    got_c = wide(move(narrow(of_c), OTHER_CORE))
    got_d = wide(move(narrow(of_d), OTHER_CORE))
    got_m2 = wide(move(narrow(of_m2), MATE_Y))
    got_ma = wide(move(narrow(of_ma), DOWN_X))
    got_mb = wide(move(narrow(of_mb), UP_X))
    got_y = wide(move(narrow(of_y + got_d), FLIP_Y))
    sum_2 = narrow(of_2 + got_m2)
    got_2a = wide(move(sum_2[:half], UP_X))
    got_2b = wide(move(sum_2[half:], DOWN_X))
    got_m = wide(move(narrow(of_m + got_ma + got_mb), MATE_Y))
    for_z = jnp.where(second, 0.0, got_c) + jnp.where(upper, 0.0, got_y)
    got_z = wide(move(narrow(for_z), UP_Z))
    zeros = jnp.zeros((half, image_embed.shape[1]), jnp.float32)
    got_a = wide(move(narrow(of_a + jnp.concatenate([zeros, got_2b], 0)), DOWN_X))
    got_b = wide(move(narrow(of_b + jnp.concatenate([got_2a, zeros], 0)), UP_X))

    loss_sum = jnp.sum(loss_part.reshape(8, -1, 128), axis=1)
    for pairs in LOSS_ROUTES:
        loss_sum = loss_sum + move(loss_sum, pairs)
    pair_loss = jnp.sum(loss_sum) / jnp.float32(image_embed.shape[0] * 256 * BAND * rows * X * YL)
    img_grad = of_own + got_a + got_b + got_m
    txt_grad = of_txt + jnp.where(second, got_c, 0.0) + jnp.where(upper, got_y, 0.0) + got_z
    return pair_loss, back_norm(image_embed, img_grad), back_norm(text_embed, txt_grad)


def solution(mesh):
    return jax.shard_map(
        shards,
        mesh=mesh,
        in_specs=(P(AXES, None), P(AXES, None), P(), P()),
        out_specs=(P(), P(AXES, None), P(AXES, None)),
        check_vma=False,
    )
```

```python
import functools

import jax
import jax.numpy as jnp
from jax import lax
from jax.experimental import pallas as pl
from jax.experimental.pallas import tpu as pltpu
from jax.sharding import PartitionSpec as P

BAND = 4
EPS = 1e-06
AXES = ("site", "dp")
Z, YH, CORE, X, YL = 8, 2, 2, 4, 2


def route(move):
    pairs = []
    for source in range(Z * YH * CORE * X * YL):
        rest, yl = divmod(source, YL)
        rest, x = divmod(rest, X)
        rest, core = divmod(rest, CORE)
        z, yh = divmod(rest, YH)
        z, yh, core, x, yl = move(z, yh, core, x, yl)
        target = ((((z % Z) * YH + yh) * CORE + core) * X + x % X) * YL + yl
        pairs.append((source, target))
    return pairs


def inverse(pairs):
    return [(target, source) for source, target in pairs]


UP_X = route(lambda z, yh, c, x, yl: (z, yh, c, x + 1, yl))
DOWN_X = route(lambda z, yh, c, x, yl: (z, yh, c, x - 1, yl))
MATE_Y = route(lambda z, yh, c, x, yl: (z, yh, c, x, 1 - yl))
OTHER_CORE = route(lambda z, yh, c, x, yl: (z, yh, 1 - c, x, yl))
SIDE = route(lambda z, yh, c, x, yl: (z - (c == 0), yh, 1 - c, x, yl))
AHEAD = route(lambda z, yh, c, x, yl: (z - (yh == 0), 1 - yh, c, x, 1 - yl))
LOSS_ROUTES = (
    OTHER_CORE,
    route(lambda z, yh, c, x, yl: (z, yh, c, x ^ 1, yl)),
    route(lambda z, yh, c, x, yl: (z, yh, c, 3 - x, yl)),
    MATE_Y,
    route(lambda z, yh, c, x, yl: (z, 1 - yh, c, x, 1 - yl)),
    route(lambda z, yh, c, x, yl: (z ^ 1, yh, c, x, yl)),
    route(lambda z, yh, c, x, yl: (z ^ 2, yh, c, x, yl)),
    route(lambda z, yh, c, x, yl: (z ^ 4, yh, c, x, yl)),
)


def move(block, pairs):
    return lax.ppermute(block, AXES, pairs)


def unit_kernel(image_ref, text_ref, img_unit_ref, txt_unit_ref):
    for source, unit in ((image_ref, img_unit_ref), (text_ref, txt_unit_ref)):
        values = source[...].astype(jnp.float32)
        inverse = lax.rsqrt(jnp.sum(values * values, axis=-1, keepdims=True) + EPS)
        unit[...] = (values * inverse).astype(jnp.bfloat16)


def units(image_embed, text_embed):
    out = jax.ShapeDtypeStruct(image_embed.shape, jnp.bfloat16)
    return pl.pallas_call(unit_kernel, out_shape=(out, out))(image_embed, text_embed)


def dot(left, right, dims):
    return lax.dot_general(left, right, ((dims[:1], dims[1:]), ((), ())), preferred_element_type=jnp.float32)


def spread(values, refs):
    start = 0
    for ref in refs:
        ref[...] = values[start : start + ref.shape[0], :]
        start += ref.shape[0]


def score_kernel(scalars_ref, *refs):
    img_refs, txt_refs, refs = refs[:9], refs[9:13], refs[13:]
    img, txt, weights, loss_ref = refs[:4]
    grad_refs = refs[4:]
    rows = txt_refs[0].shape[0]
    start = 0
    for ref in img_refs:
        img[start : start + ref.shape[0], :] = ref[...]
        start += ref.shape[0]
    for k, ref in enumerate(txt_refs):
        txt[k * rows : (k + 1) * rows, :] = ref[...]
    sharpness = scalars_ref[0]
    shift = scalars_ref[1]
    chunk = 2 * rows
    texts = txt[...]
    loss = jnp.zeros((8, texts.shape[0]), jnp.float32)
    for i in range(img.shape[0] // chunk):
        block = slice(i * chunk, (i + 1) * chunk)
        score = sharpness * dot(img[block, :], texts, (1, 1)) + shift
        decay = jnp.exp(-jnp.abs(score))
        softplus = jnp.maximum(score, 0.0) + jnp.log1p(decay)
        sigmoid = jnp.where(score >= 0, 1.0, decay) / (1.0 + decay)
        if i == 2:
            row = lax.broadcasted_iota(jnp.int32, score.shape, 0)
            column = lax.broadcasted_iota(jnp.int32, score.shape, 1)
            positive = row + 3 * rows == column
            softplus = jnp.where(positive, jnp.maximum(-score, 0.0) + jnp.log1p(decay), softplus)
            sigmoid = sigmoid - jnp.where(positive, 1.0, 0.0)
        loss = loss + jnp.sum(softplus.reshape(-1, 8, softplus.shape[1]), axis=0)
        weight = (sharpness * sigmoid).astype(jnp.bfloat16)
        weights[block, :] = weight
        if 2 * i < len(grad_refs):
            spread(dot(weight, texts, (1, 0)), grad_refs[2 * i : 2 * i + 2])
    loss_ref[...] = sum(loss[:, i * 128 : (i + 1) * 128] for i in range(texts.shape[0] // 128))


def text_kernel(weights, img, *grad_refs):
    chunk = 2 * grad_refs[0].shape[0]
    for i in range(0, len(grad_refs), 2):
        start = i // 2 * chunk
        spread(dot(weights[:, start : start + chunk], img[...], (0, 0)), grad_refs[i : i + 2])


def image_kernel(weights, txt, *grad_refs):
    chunk = 2 * grad_refs[0].shape[0]
    first = weights.shape[0] - chunk * len(grad_refs) // 2
    for i in range(0, len(grad_refs), 2):
        start = first + i // 2 * chunk
        spread(dot(weights[start : start + chunk, :], txt[...], (1, 0)), grad_refs[i : i + 2])


VMEM = pl.BlockSpec(memory_space=pltpu.VMEM)
SMEM = pl.BlockSpec(memory_space=pltpu.SMEM)
PARAMS = pltpu.CompilerParams(vmem_limit_bytes=30 * 1024 * 1024)


def grads(count, rows, width):
    return (jax.ShapeDtypeStruct((rows, width), jnp.float32),) * count


def score_terms(scalars, images, texts):
    rows, width = texts[0].shape
    img_rows, txt_rows = rows * X * YL, rows * BAND
    out_shape = (
        jax.ShapeDtypeStruct((img_rows, width), jnp.bfloat16),
        jax.ShapeDtypeStruct((txt_rows, width), jnp.bfloat16),
        jax.ShapeDtypeStruct((img_rows, txt_rows), jnp.bfloat16),
        jax.ShapeDtypeStruct((8, 128), jnp.float32),
        *grads(4, rows, width),
    )
    return pl.pallas_call(
        score_kernel,
        out_shape=out_shape,
        in_specs=[SMEM] + [VMEM] * (len(images) + len(texts)),
        out_specs=(VMEM,) * len(out_shape),
        compiler_params=PARAMS,
    )(scalars, *images, *texts)


def text_terms(weights, img, rows):
    out_shape = grads(4, rows, img.shape[1])
    return pl.pallas_call(text_kernel, out_shape=out_shape, compiler_params=PARAMS)(weights, img)


def image_terms(weights, txt, rows):
    out_shape = grads(4, rows, txt.shape[1])
    return pl.pallas_call(image_kernel, out_shape=out_shape, compiler_params=PARAMS)(weights, txt)


def final_kernel(embed_ref, upstream_ref, grad_ref):
    values = embed_ref[...].astype(jnp.float32)
    upstream = upstream_ref[...]
    inverse = lax.rsqrt(jnp.sum(values * values, axis=-1, keepdims=True) + EPS)
    inner = jnp.sum(values * upstream, axis=-1, keepdims=True)
    grad_ref[...] = inverse * upstream - inverse * inverse * inverse * values * inner


def back_norm(embed, upstream):
    return pl.pallas_call(
        final_kernel, out_shape=jax.ShapeDtypeStruct(upstream.shape, jnp.float32)
    )(embed, upstream)


def narrow(block):
    return block.astype(jnp.float16)


def wide(block):
    return block.astype(jnp.float32)


def together(*values):
    return lax.optimization_barrier(values)


def loss_step(total, index):
    return total + move(total, LOSS_ROUTES[index])


def shards(image_embed, text_embed, log_sharpness_factor, couple_score_shift):
    rows, width = image_embed.shape
    half = rows // 2
    scalars = jnp.stack([jnp.exp(log_sharpness_factor), couple_score_shift])
    own_img, own_txt = units(image_embed, text_embed)

    txt_y = move(own_txt, AHEAD)
    txt_c = move(own_txt, SIDE)
    img_m = move(own_img, MATE_Y)
    img_b = move(own_img, DOWN_X)
    img_a = move(own_img, UP_X)
    img_a, img_b, img_m = together(img_a, img_b, img_m)
    img_ma = move(img_a, MATE_Y)
    img_mb = move(img_m, DOWN_X)
    img_2 = move(img_a, UP_X)
    txt_y, txt_c, img_a2, img_mb2 = together(txt_y, txt_c, img_2, img_mb)
    txt_d = move(txt_y, OTHER_CORE)
    img_m2b = move(img_mb2[half:], DOWN_X)
    img_m2a = move(img_a2[:half], MATE_Y)

    images = (img_m2a, img_m2b, img_2, img_mb, img_ma, own_img, img_a, img_b, img_m)
    texts = (txt_c, txt_d, txt_y, own_txt)
    img, txt, weights, loss, of_m2, of_2, of_mb, of_ma = score_terms(scalars, images, texts)
    got_m2a = move(narrow(of_m2[:half]), MATE_Y)
    got_m2b = move(narrow(of_m2[half:]), UP_X)
    loss = loss_step(loss, 0)
    of_c, of_d, of_y, own_txt_grad = text_terms(weights, img, rows)
    got_d = move(narrow(of_d), OTHER_CORE)
    own_img_grad, of_a, of_b, of_m = image_terms(weights, txt, rows)
    loss, of_m = together(loss, of_m)
    loss = loss_step(loss, 1)
    got_m2a, loss = together(got_m2a, loss)
    got_m2a, got_m2b, got_d, own_img_grad = together(got_m2a, got_m2b, got_d, own_img_grad)
    zeros = jnp.zeros((half, width), jnp.float32)
    got_ma = move(narrow(of_ma), MATE_Y)
    got_2 = move(narrow(of_2 + jnp.concatenate([wide(got_m2a), zeros], 0)), DOWN_X)
    got_mb = move(narrow(of_mb + jnp.concatenate([zeros, wide(got_m2b)], 0)), UP_X)
    got_y = move(narrow(of_y + wide(got_d)), inverse(AHEAD))
    got_c = move(narrow(of_c), inverse(SIDE))
    loss = loss_step(loss, 2)
    loss = loss_step(loss, 3)
    got_ma, loss = together(got_ma, loss)
    got_ma, got_2, got_mb = together(got_ma, got_2, got_mb)
    got_b = move(narrow(of_b), UP_X)
    got_m = move(narrow(of_m + wide(got_mb)), MATE_Y)
    got_a = move(narrow(of_a + wide(got_2) + wide(got_ma)), DOWN_X)
    loss = loss_step(loss, 4)
    loss = loss_step(loss, 5)
    got_y, loss = together(got_y, loss)
    got_y, got_c = together(got_y, got_c)
    txt_grad = own_txt_grad + wide(got_c) + wide(got_y)
    grad_text = back_norm(text_embed, txt_grad)
    got_a, got_b, got_m, grad_text = together(got_a, got_b, got_m, grad_text)
    loss = loss_step(loss, 6)
    loss = loss_step(loss, 7)
    img_grad = own_img_grad + wide(got_a) + wide(got_b) + wide(got_m)
    grad_image = back_norm(image_embed, img_grad)
    pair_loss = jnp.sum(loss) / jnp.float32(rows * 256 * BAND * rows * X * YL)
    return pair_loss, grad_image, grad_text


def solution(mesh):
    return jax.shard_map(
        shards,
        mesh=mesh,
        in_specs=(P(AXES, None), P(AXES, None), P(), P()),
        out_specs=(P(), P(AXES, None), P(AXES, None)),
        check_vma=False,
    )
```

```python
import functools

import jax
import jax.numpy as jnp
from jax import lax
from jax.experimental import pallas as pl
from jax.experimental.pallas import tpu as pltpu
from jax.sharding import PartitionSpec as P

BAND = 4
EPS = 1e-06
AXES = ("site", "dp")
Z, YH, CORE, X, YL = 8, 2, 2, 4, 2


def route(move):
    pairs = []
    for source in range(Z * YH * CORE * X * YL):
        rest, yl = divmod(source, YL)
        rest, x = divmod(rest, X)
        rest, core = divmod(rest, CORE)
        z, yh = divmod(rest, YH)
        z, yh, core, x, yl = move(z, yh, core, x, yl)
        target = ((((z % Z) * YH + yh) * CORE + core) * X + x % X) * YL + yl
        pairs.append((source, target))
    return pairs


def inverse(pairs):
    return [(target, source) for source, target in pairs]


UP_X = route(lambda z, yh, c, x, yl: (z, yh, c, x + 1, yl))
DOWN_X = route(lambda z, yh, c, x, yl: (z, yh, c, x - 1, yl))
MATE_Y = route(lambda z, yh, c, x, yl: (z, yh, c, x, 1 - yl))
OTHER_CORE = route(lambda z, yh, c, x, yl: (z, yh, 1 - c, x, yl))
SIDE = route(lambda z, yh, c, x, yl: (z - (c == 0), yh, 1 - c, x, yl))
AHEAD = route(lambda z, yh, c, x, yl: (z - (yh == 0), 1 - yh, c, x, 1 - yl))
LOSS_ROUTES = (
    OTHER_CORE,
    route(lambda z, yh, c, x, yl: (z, yh, c, x ^ 1, yl)),
    route(lambda z, yh, c, x, yl: (z, yh, c, 3 - x, yl)),
    MATE_Y,
    route(lambda z, yh, c, x, yl: (z, 1 - yh, c, x, 1 - yl)),
    route(lambda z, yh, c, x, yl: (z ^ 1, yh, c, x, yl)),
    route(lambda z, yh, c, x, yl: (z ^ 2, yh, c, x, yl)),
    route(lambda z, yh, c, x, yl: (z ^ 4, yh, c, x, yl)),
)


def move(block, pairs):
    return lax.ppermute(block, AXES, pairs)


def unit_kernel(embed_ref, unit_ref):
    values = embed_ref[...].astype(jnp.float32)
    inverse = lax.rsqrt(jnp.sum(values * values, axis=-1, keepdims=True) + EPS)
    unit_ref[...] = (values * inverse).astype(jnp.bfloat16)


def unit(embed):
    out_shape = jax.ShapeDtypeStruct(embed.shape, jnp.bfloat16)
    return pl.pallas_call(unit_kernel, out_shape=out_shape, compiler_params=SMALL)(embed)


def dot(left, right, dims):
    return lax.dot_general(left, right, ((dims[:1], dims[1:]), ((), ())), preferred_element_type=jnp.float32)


def spread(values, refs):
    start = 0
    for ref in refs:
        ref[...] = values[start : start + ref.shape[0], :]
        start += ref.shape[0]


def score_kernel(scalars_ref, *refs):
    img_refs, txt_refs, refs = refs[:8], refs[8:12], refs[12:]
    img, txt, weights, loss_ref = refs[:4]
    grad_refs = refs[4:]
    rows = txt_refs[0].shape[0]
    start = 0
    for ref in img_refs:
        img[start : start + ref.shape[0], :] = ref[...]
        start += ref.shape[0]
    for k, ref in enumerate(txt_refs):
        txt[k * rows : (k + 1) * rows, :] = ref[...]
    sharpness = scalars_ref[0]
    shift = scalars_ref[1]
    chunk = 2 * rows
    texts = txt[...]
    loss = jnp.zeros((8, texts.shape[0]), jnp.float32)
    for i in range(img.shape[0] // chunk):
        block = slice(i * chunk, (i + 1) * chunk)
        score = sharpness * dot(img[block, :], texts, (1, 1)) + shift
        decay = jnp.exp(-jnp.abs(score))
        softplus = jnp.maximum(score, 0.0) + jnp.log1p(decay)
        sigmoid = jnp.where(score >= 0, 1.0, decay) / (1.0 + decay)
        if i == 2:
            row = lax.broadcasted_iota(jnp.int32, score.shape, 0)
            column = lax.broadcasted_iota(jnp.int32, score.shape, 1)
            positive = row + 3 * rows == column
            softplus = jnp.where(positive, jnp.maximum(-score, 0.0) + jnp.log1p(decay), softplus)
            sigmoid = sigmoid - jnp.where(positive, 1.0, 0.0)
        loss = loss + jnp.sum(softplus.reshape(-1, 8, softplus.shape[1]), axis=0)
        weight = (sharpness * sigmoid).astype(jnp.bfloat16)
        weights[block, :] = weight
        if 2 * i < len(grad_refs):
            spread(dot(weight, texts, (1, 0)), grad_refs[2 * i : 2 * i + 2])
    loss_ref[...] = sum(loss[:, i * 128 : (i + 1) * 128] for i in range(texts.shape[0] // 128))


def text_kernel(weights, img, *grad_refs):
    chunk = 2 * grad_refs[0].shape[0]
    for i in range(0, len(grad_refs), 2):
        start = i // 2 * chunk
        spread(dot(weights[:, start : start + chunk], img[...], (0, 0)), grad_refs[i : i + 2])


def image_kernel(weights, txt, *grad_refs):
    chunk = 2 * grad_refs[0].shape[0]
    first = weights.shape[0] - chunk * len(grad_refs) // 2
    for i in range(0, len(grad_refs), 2):
        start = first + i // 2 * chunk
        spread(dot(weights[start : start + chunk, :], txt[...], (1, 0)), grad_refs[i : i + 2])


VMEM = pl.BlockSpec(memory_space=pltpu.VMEM)
SMEM = pl.BlockSpec(memory_space=pltpu.SMEM)
LARGE = pltpu.CompilerParams(vmem_limit_bytes=16 * 1024 * 1024)
SMALL = pltpu.CompilerParams(vmem_limit_bytes=4 * 1024 * 1024)


def grads(count, rows, width):
    return (jax.ShapeDtypeStruct((rows, width), jnp.float32),) * count


def score_terms(scalars, images, texts):
    rows, width = texts[0].shape
    img_rows, txt_rows = rows * X * YL, rows * BAND
    out_shape = (
        jax.ShapeDtypeStruct((img_rows, width), jnp.bfloat16),
        jax.ShapeDtypeStruct((txt_rows, width), jnp.bfloat16),
        jax.ShapeDtypeStruct((img_rows, txt_rows), jnp.bfloat16),
        jax.ShapeDtypeStruct((8, 128), jnp.float32),
        *grads(4, rows, width),
    )
    return pl.pallas_call(
        score_kernel,
        out_shape=out_shape,
        in_specs=[SMEM] + [VMEM] * (len(images) + len(texts)),
        out_specs=(VMEM,) * len(out_shape),
        compiler_params=LARGE,
    )(scalars, *images, *texts)


def text_terms(weights, img, rows):
    out_shape = grads(4, rows, img.shape[1])
    return pl.pallas_call(text_kernel, out_shape=out_shape, compiler_params=LARGE)(weights, img)


def image_terms(weights, txt, rows):
    out_shape = grads(4, rows, txt.shape[1])
    return pl.pallas_call(image_kernel, out_shape=out_shape, compiler_params=LARGE)(weights, txt)


def final_kernel(embed_ref, upstream_ref, grad_ref):
    values = embed_ref[...].astype(jnp.float32)
    upstream = upstream_ref[...]
    inverse = lax.rsqrt(jnp.sum(values * values, axis=-1, keepdims=True) + EPS)
    inner = jnp.sum(values * upstream, axis=-1, keepdims=True)
    grad_ref[...] = inverse * upstream - inverse * inverse * inverse * values * inner


def back_norm(embed, upstream):
    return pl.pallas_call(
        final_kernel,
        out_shape=jax.ShapeDtypeStruct(upstream.shape, jnp.float32),
        compiler_params=SMALL,
    )(embed, upstream)


def narrow(block):
    return block.astype(jnp.float16)


def wide(block):
    return block.astype(jnp.float32)


def together(*values):
    return lax.optimization_barrier(values)


def loss_step(total, index):
    return total + move(total, LOSS_ROUTES[index])


def shards(image_embed, text_embed, log_sharpness_factor, couple_score_shift):
    rows, width = image_embed.shape
    scalars = jnp.stack([jnp.exp(log_sharpness_factor), couple_score_shift])
    own_img = unit(image_embed)
    own_txt = unit(text_embed)

    txt_y = move(own_txt, AHEAD)
    txt_c = move(own_txt, SIDE)
    img_m = move(own_img, MATE_Y)
    img_b = move(own_img, DOWN_X)
    img_a = move(own_img, UP_X)
    img_a, img_b, img_m = together(img_a, img_b, img_m)
    img_ma = move(img_a, MATE_Y)
    img_mb = move(img_m, DOWN_X)
    img_2 = move(img_a, UP_X)
    txt_y, txt_c, img_2 = together(txt_y, txt_c, img_2)
    txt_d = move(txt_y, OTHER_CORE)
    img_m2 = move(img_2, MATE_Y)
    images = (img_m2, img_2, img_mb, img_ma, own_img, img_a, img_b, img_m)
    texts = (txt_c, txt_d, txt_y, own_txt)
    img, txt, weights, loss, of_m2, of_2, of_mb, of_ma = score_terms(scalars, images, texts)
    got_m2 = move(narrow(of_m2), MATE_Y)
    got_mb = move(narrow(of_mb), UP_X)
    loss = loss_step(loss, 0)
    of_c, of_d, of_y, own_txt_grad = text_terms(weights, img, rows)
    got_d = move(narrow(of_d), OTHER_CORE)
    got_ma = move(narrow(of_ma), MATE_Y)
    own_img_grad, of_a, of_b, of_m = image_terms(weights, txt, rows)
    loss, of_m = together(loss, of_m)
    loss = loss_step(loss, 1)
    got_m2, loss = together(got_m2, loss)
    got_m2, got_mb, got_d, own_img_grad = together(got_m2, got_mb, got_d, own_img_grad)
    got_2 = move(narrow(of_2 + wide(got_m2)), DOWN_X)
    got_y = move(narrow(of_y + wide(got_d)), inverse(AHEAD))
    got_c = move(narrow(of_c), inverse(SIDE))
    got_m = move(narrow(of_m + wide(got_mb)), MATE_Y)
    loss = loss_step(loss, 2)
    loss = loss_step(loss, 3)
    got_ma, loss = together(got_ma, loss)
    got_ma, got_2, of_b = together(got_ma, got_2, of_b)
    got_b = move(narrow(of_b), UP_X)
    got_a = move(narrow(of_a + wide(got_2) + wide(got_ma)), DOWN_X)
    loss = loss_step(loss, 4)
    loss = loss_step(loss, 5)
    got_y, loss = together(got_y, loss)
    got_y, got_c = together(got_y, got_c)
    txt_grad = own_txt_grad + wide(got_c) + wide(got_y)
    grad_text = back_norm(text_embed, txt_grad)
    got_a, got_b, got_m, grad_text = together(got_a, got_b, got_m, grad_text)
    loss = loss_step(loss, 6)
    loss = loss_step(loss, 7)
    img_grad = own_img_grad + wide(got_a) + wide(got_b) + wide(got_m)
    grad_image = back_norm(image_embed, img_grad)
    loss, grad_image = together(loss, grad_image)
    pair_loss = jnp.sum(loss) / jnp.float32(rows * 256 * BAND * rows * X * YL)
    return pair_loss, grad_image, grad_text


def solution(mesh):
    return jax.shard_map(
        shards,
        mesh=mesh,
        in_specs=(P(AXES, None), P(AXES, None), P(), P()),
        out_specs=(P(), P(AXES, None), P(AXES, None)),
        check_vma=False,
    )
```

```python
import functools

import jax
import jax.numpy as jnp
from jax import lax
from jax.experimental import pallas as pl
from jax.experimental.pallas import tpu as pltpu
from jax.sharding import PartitionSpec as P

BAND = 4
EPS = 1e-06
AXES = ("site", "dp")
Z, YH, CORE, X, YL = 8, 2, 2, 4, 2


def route(move):
    pairs = []
    for source in range(Z * YH * CORE * X * YL):
        rest, yl = divmod(source, YL)
        rest, x = divmod(rest, X)
        rest, core = divmod(rest, CORE)
        z, yh = divmod(rest, YH)
        z, yh, core, x, yl = move(z, yh, core, x, yl)
        target = ((((z % Z) * YH + yh) * CORE + core) * X + x % X) * YL + yl
        pairs.append((source, target))
    return pairs


def inverse(pairs):
    return [(target, source) for source, target in pairs]


UP_X = route(lambda z, yh, c, x, yl: (z, yh, c, x + 1, yl))
DOWN_X = route(lambda z, yh, c, x, yl: (z, yh, c, x - 1, yl))
MATE_Y = route(lambda z, yh, c, x, yl: (z, yh, c, x, 1 - yl))
OTHER_CORE = route(lambda z, yh, c, x, yl: (z, yh, 1 - c, x, yl))
SIDE = route(lambda z, yh, c, x, yl: (z - (c == 0), yh, 1 - c, x, yl))
AHEAD = route(lambda z, yh, c, x, yl: (z - (yh == 0), 1 - yh, c, x, 1 - yl))
LOSS_ROUTES = (
    OTHER_CORE,
    route(lambda z, yh, c, x, yl: (z, yh, c, x ^ 1, yl)),
    route(lambda z, yh, c, x, yl: (z, yh, c, 3 - x, yl)),
    MATE_Y,
    route(lambda z, yh, c, x, yl: (z, 1 - yh, c, x, 1 - yl)),
    route(lambda z, yh, c, x, yl: (z ^ 1, yh, c, x, yl)),
    route(lambda z, yh, c, x, yl: (z ^ 2, yh, c, x, yl)),
    route(lambda z, yh, c, x, yl: (z ^ 4, yh, c, x, yl)),
)


def quad(total, pairs):
    first, second, third = (move(total, route) for route in pairs)
    return (total + first) + (second + third)


X_QUAD = (
    route(lambda z, yh, c, x, yl: (z, yh, c, x ^ 1, yl)),
    route(lambda z, yh, c, x, yl: (z, yh, c, x ^ 2, yl)),
    route(lambda z, yh, c, x, yl: (z, yh, c, x ^ 3, yl)),
)
Y_QUAD = (
    MATE_Y,
    route(lambda z, yh, c, x, yl: (z, 1 - yh, c, x, yl)),
    route(lambda z, yh, c, x, yl: (z, 1 - yh, c, x, 1 - yl)),
)
Z_QUAD = (
    route(lambda z, yh, c, x, yl: (z ^ 1, yh, c, x, yl)),
    route(lambda z, yh, c, x, yl: (z ^ 2, yh, c, x, yl)),
    route(lambda z, yh, c, x, yl: (z ^ 3, yh, c, x, yl)),
)


def move(block, pairs):
    return lax.ppermute(block, AXES, pairs)


def unit_kernel(embed_ref, unit_ref):
    values = embed_ref[...].astype(jnp.float32)
    inverse = lax.rsqrt(jnp.sum(values * values, axis=-1, keepdims=True) + EPS)
    unit_ref[...] = (values * inverse).astype(jnp.bfloat16)


def unit(embed):
    out_shape = jax.ShapeDtypeStruct(embed.shape, jnp.bfloat16)
    return pl.pallas_call(unit_kernel, out_shape=out_shape, compiler_params=SMALL)(embed)


def dot(left, right, dims):
    return lax.dot_general(left, right, ((dims[:1], dims[1:]), ((), ())), preferred_element_type=jnp.float32)


def spread(values, refs):
    start = 0
    for ref in refs:
        ref[...] = values[start : start + ref.shape[0], :]
        start += ref.shape[0]


def score_kernel(scalars_ref, *refs):
    img_refs, txt_refs, refs = refs[:8], refs[8:12], refs[12:]
    img, txt, weights, loss_ref = refs[:4]
    grad_refs = refs[4:]
    rows = txt_refs[0].shape[0]
    start = 0
    for ref in img_refs:
        img[start : start + ref.shape[0], :] = ref[...]
        start += ref.shape[0]
    for k, ref in enumerate(txt_refs):
        txt[k * rows : (k + 1) * rows, :] = ref[...]
    sharpness = scalars_ref[0]
    shift = scalars_ref[1]
    chunk = 2 * rows
    texts = txt[...]
    loss = jnp.zeros((8, texts.shape[0]), jnp.float32)
    for i in range(img.shape[0] // chunk):
        block = slice(i * chunk, (i + 1) * chunk)
        score = sharpness * dot(img[block, :], texts, (1, 1)) + shift
        decay = jnp.exp(-jnp.abs(score))
        softplus = jnp.maximum(score, 0.0) + jnp.log1p(decay)
        sigmoid = jnp.where(score >= 0, 1.0, decay) / (1.0 + decay)
        if i == 2:
            row = lax.broadcasted_iota(jnp.int32, score.shape, 0)
            column = lax.broadcasted_iota(jnp.int32, score.shape, 1)
            positive = row + 3 * rows == column
            softplus = jnp.where(positive, jnp.maximum(-score, 0.0) + jnp.log1p(decay), softplus)
            sigmoid = sigmoid - jnp.where(positive, 1.0, 0.0)
        loss = loss + jnp.sum(softplus.reshape(-1, 8, softplus.shape[1]), axis=0)
        weight = (sharpness * sigmoid).astype(jnp.bfloat16)
        weights[block, :] = weight
        if 2 * i < len(grad_refs):
            spread(dot(weight, texts, (1, 0)), grad_refs[2 * i : 2 * i + 2])
    loss_ref[...] = sum(loss[:, i * 128 : (i + 1) * 128] for i in range(texts.shape[0] // 128))


def text_kernel(weights, img, *grad_refs):
    chunk = 2 * grad_refs[0].shape[0]
    for i in range(0, len(grad_refs), 2):
        start = i // 2 * chunk
        spread(dot(weights[:, start : start + chunk], img[...], (0, 0)), grad_refs[i : i + 2])


def image_kernel(weights, txt, *grad_refs):
    chunk = 2 * grad_refs[0].shape[0]
    first = weights.shape[0] - chunk * len(grad_refs) // 2
    for i in range(0, len(grad_refs), 2):
        start = first + i // 2 * chunk
        spread(dot(weights[start : start + chunk, :], txt[...], (1, 0)), grad_refs[i : i + 2])


VMEM = pl.BlockSpec(memory_space=pltpu.VMEM)
SMEM = pl.BlockSpec(memory_space=pltpu.SMEM)
LARGE = pltpu.CompilerParams(vmem_limit_bytes=16 * 1024 * 1024)
SMALL = pltpu.CompilerParams(vmem_limit_bytes=4 * 1024 * 1024)


def grads(count, rows, width):
    return (jax.ShapeDtypeStruct((rows, width), jnp.float32),) * count


def score_terms(scalars, images, texts):
    rows, width = texts[0].shape
    img_rows, txt_rows = rows * X * YL, rows * BAND
    out_shape = (
        jax.ShapeDtypeStruct((img_rows, width), jnp.bfloat16),
        jax.ShapeDtypeStruct((txt_rows, width), jnp.bfloat16),
        jax.ShapeDtypeStruct((img_rows, txt_rows), jnp.bfloat16),
        jax.ShapeDtypeStruct((8, 128), jnp.float32),
        *grads(4, rows, width),
    )
    return pl.pallas_call(
        score_kernel,
        out_shape=out_shape,
        in_specs=[SMEM] + [VMEM] * (len(images) + len(texts)),
        out_specs=(VMEM,) * len(out_shape),
        compiler_params=LARGE,
    )(scalars, *images, *texts)


def text_terms(weights, img, rows):
    out_shape = grads(4, rows, img.shape[1])
    return pl.pallas_call(text_kernel, out_shape=out_shape, compiler_params=LARGE)(weights, img)


def image_terms(weights, txt, rows):
    out_shape = grads(4, rows, txt.shape[1])
    return pl.pallas_call(image_kernel, out_shape=out_shape, compiler_params=LARGE)(weights, txt)


def final_kernel(embed_ref, upstream_ref, grad_ref):
    values = embed_ref[...].astype(jnp.float32)
    upstream = upstream_ref[...]
    inverse = lax.rsqrt(jnp.sum(values * values, axis=-1, keepdims=True) + EPS)
    inner = jnp.sum(values * upstream, axis=-1, keepdims=True)
    grad_ref[...] = inverse * upstream - inverse * inverse * inverse * values * inner


def back_norm(embed, upstream):
    return pl.pallas_call(
        final_kernel,
        out_shape=jax.ShapeDtypeStruct(upstream.shape, jnp.float32),
        compiler_params=SMALL,
    )(embed, upstream)


def narrow(block):
    return block.astype(jnp.float16)


def wide(block):
    return block.astype(jnp.float32)


def together(*values):
    return lax.optimization_barrier(values)


def loss_step(total, index):
    return total + move(total, LOSS_ROUTES[index])


def shards(image_embed, text_embed, log_sharpness_factor, couple_score_shift):
    rows, width = image_embed.shape
    scalars = jnp.stack([jnp.exp(log_sharpness_factor), couple_score_shift])
    own_img = unit(image_embed)
    own_txt = unit(text_embed)

    txt_y = move(own_txt, AHEAD)
    txt_c = move(own_txt, SIDE)
    img_m = move(own_img, MATE_Y)
    img_b = move(own_img, DOWN_X)
    img_a = move(own_img, UP_X)
    img_a, img_b, img_m = together(img_a, img_b, img_m)
    img_ma = move(img_a, MATE_Y)
    img_mb = move(img_m, DOWN_X)
    img_2 = move(img_a, UP_X)
    txt_y, txt_c, img_2 = together(txt_y, txt_c, img_2)
    txt_d = move(txt_y, OTHER_CORE)
    img_m2 = move(img_2, MATE_Y)
    images = (img_m2, img_2, img_mb, img_ma, own_img, img_a, img_b, img_m)
    texts = (txt_c, txt_d, txt_y, own_txt)
    img, txt, weights, loss, of_m2, of_2, of_mb, of_ma = score_terms(scalars, images, texts)
    got_m2 = move(narrow(of_m2), MATE_Y)
    got_mb = move(narrow(of_mb), UP_X)
    loss = loss_step(loss, 0)
    of_c, of_d, of_y, own_txt_grad = text_terms(weights, img, rows)
    got_d = move(narrow(of_d), OTHER_CORE)
    got_ma = move(narrow(of_ma), MATE_Y)
    own_img_grad, of_a, of_b, of_m = image_terms(weights, txt, rows)
    loss, of_m = together(loss, of_m)
    loss = loss_step(loss, 1)
    got_m2, loss = together(got_m2, loss)
    got_m2, got_mb, got_d, own_img_grad = together(got_m2, got_mb, got_d, own_img_grad)
    got_2 = move(narrow(of_2 + wide(got_m2)), DOWN_X)
    got_y = move(narrow(of_y + wide(got_d)), inverse(AHEAD))
    got_c = move(narrow(of_c), inverse(SIDE))
    got_m = move(narrow(of_m + wide(got_mb)), MATE_Y)
    loss = loss_step(loss, 2)
    loss = loss_step(loss, 3)
    got_ma, loss = together(got_ma, loss)
    got_ma, got_2, of_b = together(got_ma, got_2, of_b)
    got_b = move(narrow(of_b), UP_X)
    got_a = move(narrow(of_a + wide(got_2) + wide(got_ma)), DOWN_X)
    loss = loss_step(loss, 4)
    got_y, loss = together(got_y, loss)
    got_y, got_c = together(got_y, got_c)
    txt_grad = own_txt_grad + wide(got_c) + wide(got_y)
    grad_text = back_norm(text_embed, txt_grad)
    got_a, got_b, got_m, grad_text = together(got_a, got_b, got_m, grad_text)
    loss = quad(loss, Z_QUAD)
    loss = loss_step(loss, 7)
    img_grad = own_img_grad + wide(got_a) + wide(got_b) + wide(got_m)
    grad_image = back_norm(image_embed, img_grad)
    loss, grad_image = together(loss, grad_image)
    pair_loss = jnp.sum(loss) / jnp.float32(rows * 256 * BAND * rows * X * YL)
    return pair_loss, grad_image, grad_text


def solution(mesh):
    return jax.shard_map(
        shards,
        mesh=mesh,
        in_specs=(P(AXES, None), P(AXES, None), P(), P()),
        out_specs=(P(), P(AXES, None), P(AXES, None)),
        check_vma=False,
    )
```
